256 devices in a mesh: rep: 16 (over y, z_lo, core), dp: 16 (over z_hi, x).
Axes of the slice: x: 4, y: 4, z: 8 (z_hi: 4, z_lo: 2; z = z_hi * 2 + z_lo), core: 2. Of those that a mesh axis runs over, the one named last changes fastest.
Arguments:
- inputs: bfloat16 [32768, 8192], P(('rep', 'dp')), may hold values from -6 to 6
- cotangent: bfloat16 [32768, 1024], P(('rep', 'dp')), may hold values from -6 to 6
- kv_weight: bfloat16 [8192, 1024], P('dp'), may hold values from -0.1875 to 0.1875
- basis: bfloat16 [8192, 512], P('dp'), may hold values from -0.0625 to 0.0625
- moment_first: float32 [512, 1024], P(('rep', 'dp')), may hold values from -6 to 6
- moment_second: float32 [512, 1024], P(('rep', 'dp')), may hold values from 0.05 to 1
Outputs:
- input_grad: bfloat16 [32768, 8192], P(('rep', 'dp'))
- full_update: bfloat16 [8192, 1024], P('dp')
- proj_grad: float32 [512, 1024], P(('rep', 'dp'))
- first_new: float32 [512, 1024], P(('rep', 'dp'))
- second_new: float32 [512, 1024], P(('rep', 'dp'))
The draws below stay inside these ranges and needn't reach their ends.
All inputs are finite; a program needn't handle non-finite values.
Results may differ from the reference program's by a relative error of at most 0.005.
Values may be sent and summed in bfloat16 or wider, within the bound.
A program may use at most 64 MiB of HBM per device.

```python
import math
import jax
import jax.numpy as jnp

D = 8192
KV = 1024
R = 512
STEP = 20
TOKENS = 32768


def block_scale(stream_key, extent, cuts, smallest, top_value):
    def one(axis_at, parts):
        heights = jax.random.uniform(jax.random.fold_in(jax.random.fold_in(stream_key, 6), axis_at), (parts,), jnp.float32, smallest / len(cuts), top_value / len(cuts))
        return jnp.repeat(jnp.exp(heights), extent[axis_at] // parts).reshape((-1,) + (1,) * (len(extent) - axis_at - 1))

    factor_of = one(*cuts[0])
    for cut in cuts[1:]:
        factor_of = factor_of * one(*cut)
    return factor_of


def scatter_about(own_key, extent, deviation, reach, shards=(), dtype=jnp.bfloat16):
    entries = deviation * jax.random.normal(own_key, extent, jnp.float32)
    if shards:
        entries = entries * block_scale(own_key, extent, shards, -0.22, 0.18)
    return jnp.clip(entries, -reach, reach).astype(dtype)


def setup_inputs(seed: int = 0) -> dict:
    key_list = jax.random.split(jax.random.key(seed), 7)
    inputs = scatter_about(key_list[0], (TOKENS, D), 1.0, 6.0, ((0, 256),))
    cotangent = scatter_about(key_list[1], (TOKENS, KV), 1.0, 6.0, ((0, 256),))
    kv_weight = scatter_about(key_list[2], (D, KV), KV ** -0.5, 0.1875, ((0, 16),))
    basis = scatter_about(key_list[3], (D, R), D ** -0.5, 0.0625, ((0, 16),))
    moment_first = scatter_about(key_list[4], (R, KV), 1.0, 6.0, ((0, 256),), jnp.float32)
    moment_second = jnp.clip(jnp.exp(math.log(1.0) - 2.9957323 * jax.random.uniform(key_list[5], (R, KV), jnp.float32) ** block_scale(key_list[5], (R, KV), ((0, 256),), -0.2, 0.2)), 0.05, 1.0)
    return dict(inputs=inputs, cotangent=cotangent, kv_weight=kv_weight, basis=basis, moment_first=moment_first, moment_second=moment_second)


def reference(inputs, cotangent, kv_weight, basis, moment_first, moment_second):
    input_grad = jnp.dot(cotangent, kv_weight.T, preferred_element_type=jnp.float32).astype(jnp.bfloat16)
    projected = jnp.dot(inputs, basis, preferred_element_type=jnp.float32).astype(jnp.bfloat16)
    proj_grad = jnp.dot(projected.T, cotangent, preferred_element_type=jnp.float32) * float(TOKENS) ** (-0.5)
    first_new = 0.9 * moment_first + 0.1 * proj_grad
    second_new = 0.999 * moment_second + 0.001 * proj_grad * proj_grad
    mean_hat = first_new / (1.0 - 0.9 ** STEP)
    var_hat = second_new / (1.0 - 0.999 ** STEP)
    direction = (mean_hat / (jnp.sqrt(var_hat) + 1e-08)).astype(jnp.bfloat16)
    full_update = jnp.dot(basis, direction, preferred_element_type=jnp.float32).astype(jnp.bfloat16)
    return (input_grad, full_update, proj_grad, first_new, second_new)
```

```python
import functools

import jax
import jax.numpy as jnp
from jax import lax
from jax.experimental import pallas as pl
from jax.experimental.pallas import tpu as pltpu
from jax.sharding import PartitionSpec as P

MESH = pl.DeviceIdType.MESH
STEP = 20
TOKENS = 32768
LAG = 2
F32 = jnp.float32
BF16 = jnp.bfloat16


def device(x, y, z, c):
    return ((y % 4) * 4 + (z % 2) * 2 + c, ((z % 8) // 2) * 4 + x % 4)


def kernel(
    x_ref, cot_ref, kv_ref, basis_ref, m1_ref, m2_ref,
    out_ref, fu_ref, pg_ref, first_ref, second_ref,
    xq, xr, cots, wb, wk, mom, pt, pf, sib, ysum, ysend, yr, zr, xx, dz, d64, dall, osend, orecv,
    send_sem, recv_sem,
):
    rep, dp = lax.axis_index("rep"), lax.axis_index("dp")
    c, zl, y = rep % 2, (rep // 2) % 2, rep // 4
    zh, x = dp // 4, dp % 4
    z = zh * 2 + zl
    e = y % 2
    q = e * 2 + c
    dy = 1 - 2 * c + 4
    sigma = 2 * zl - 1 + 4
    half = 1 - zl
    zlab = [zh, (zh + sigma) % 4, (zh + 8 - sigma) % 4, (zh + 2) % 4]
    xlab = [x, (x + 3) % 4, (x + 1) % 4, (x + 2) % 4]
    outer = device(x, y, z + 8 + 2 * zl - 1, c)
    inner = device(x, y, z + 1 - 2 * zl, c)
    right, left = device(x + 1, y, z, c), device(x + 3, y, z, c)
    sibling = device(x, y, z, 1 - c)
    ahead_same = device(x, y + dy, z, c)
    ahead_other = device(x, y + dy, z, 1 - c)
    behind_same = device(x, y + 8 - dy, z, c)
    behind_other = device(x, y + 8 - dy, z, 1 - c)

    barrier = pltpu.get_barrier_semaphore()
    friends = [sibling, ahead_same, ahead_other, behind_same, behind_other, device(x, y + 2, z, c)]
    friends += [device(x + k, y, z, c) for k in (1, 2, 3)]
    friends += [device(x, y, z + k, c) for k in range(1, 8)]
    for friend in friends:
        pl.semaphore_signal(barrier, inc=1, device_id=friend, device_id_type=MESH)

    for k in range(4):
        for s in range(16):
            xq[k, :, s * 128 : s * 128 + 128] = x_ref[:, s * 512 + k * 128 : s * 512 + k * 128 + 128]
    mine = zh * 4 + x
    quarter = pl.ds(pl.multiple_of(q * 128, 128), 128)
    wb[mine] = basis_ref[quarter, :]
    wk[mine] = kv_ref[quarter, :]
    cots[0] = cot_ref[...]
    mom[0, x] = m1_ref[...]
    mom[1, x] = m2_ref[...]
    pl.semaphore_wait(barrier, len(friends))

    copies = {}

    def send(name, src, dst, target):
        k = len(copies)
        copy = pltpu.make_async_remote_copy(
            src_ref=src, dst_ref=dst, send_sem=send_sem.at[k], recv_sem=recv_sem.at[k],
            device_id=target, device_id_type=MESH,
        )
        copy.start()
        copies[name] = copy

    def got(*name):
        copies[name].wait_recv()

    weights = (wb, wk)

    def piece(w, zi, xi, row, rows):
        return weights[w].at[zlab[zi] * 4 + xlab[xi], pl.ds(row, rows)]

    def push(name, w, zi, xi, row, rows, target):
        ref = piece(w, zi, xi, row, rows)
        send(name, ref, ref, target)

    def z_step(w, base, xi, step):
        n = (w, base, xi)
        lower = pl.multiple_of(base + 32 * half, 32)
        upper = pl.multiple_of(base + 32 - 32 * half, 32)
        if step == 1:
            push(n + ("z1",), w, 0, xi, base, 64, outer)
        elif step == 2:
            got(*n, "z1")
            push(n + ("z2",), w, 1, xi, base, 64, inner)
        elif step == 3:
            got(*n, "z2")
            push(n + ("z3",), w, 2, xi, lower, 32, outer)
        elif step == 4:
            got(*n, "z3")
            push(n + ("z4",), w, 3, xi, upper, 32, inner)
        else:
            got(*n, "z4")

    def x_step(w, base, zi, step):
        n = (w, base, zi)
        if step == 1:
            push(n + ("p1",), w, zi, 0, base, 64, right)
            push(n + ("m1",), w, zi, 0, base, 64, left)
        elif step == 2:
            got(*n, "p1")
            push(n + ("p2",), w, zi, 1, base, 32, right)
            got(*n, "m1")
            push(n + ("m2",), w, zi, 2, base + 32, 32, left)
        else:
            got(*n, "p2")
            got(*n, "m2")

    levels = [[] for _ in range(7)]
    for k in range(1, 6):
        levels[k - 1].append((z_step, 0, 0, k))
    for zi, ready in enumerate((0, 1, 2, 4)):
        for k in range(1, 4):
            levels[ready + k - 1].append((x_step, 0, zi, k))
    for k in range(1, 4):
        levels[k - 1].append((x_step, 64, 0, k))
    for xi, ready in enumerate((0, 1, 1, 2)):
        for k in range(1, 6):
            levels[ready + k - 1].append((z_step, 64, xi, k))

    def level(w, at):
        for step, base, label, k in levels[at]:
            step(w, base, label, k)

    other = 2 - 2 * e
    send("c_near", cot_ref, cots.at[2], ahead_same)
    send("x_near", xq.at[other + c], xr.at[2], ahead_same)
    send("x_cross", xq.at[other + 1 - c], xr.at[3], ahead_other)
    level(0, 0)
    send("x_sib", xq.at[e * 2 + 1 - c], xr.at[1], sibling)
    send("c_sib", cot_ref, cots.at[1], sibling)
    for k in (1, 2, 3):
        for j, ref in enumerate((m1_ref, m2_ref)):
            send(("m", j, k), ref, mom.at[j, x], device(x + k, y, z, c))
    level(1, 0)

    forwarded = False
    for at in range(1, 7):
        level(0, at)
        if at == 4:
            got_near = copies["c_near"]
            got_near.wait_recv()
            send("c_cross", cots.at[2], cots.at[3], sibling)
        if at - LAG >= 1:
            level(1, at - LAG)

    for name in ("x_sib", "x_near", "x_cross"):
        copies[name].wait_recv()
    xr[0] = xq[q]
    projected = jnp.dot(
        xr[...].reshape(512, 2048), wb[...].reshape(2048, 512), preferred_element_type=F32
    )
    pt[...] = projected.T.astype(BF16)
    for name in ("c_sib", "c_cross"):
        copies[name].wait_recv()
    scale = float(TOKENS) ** -0.5
    for d in (2, 1, 3, 0):
        rows = pl.ds(pl.multiple_of(((y + d) % 4) * 128, 128), 128)
        block = scale * jnp.dot(pt[rows, :], cots[...].reshape(512, 1024), preferred_element_type=F32)
        for k in range(2):
            pf[d, k, 0:32] = block[k * 32 : k * 32 + 32]
            pf[d, k, 32:64] = block[64 + k * 32 : 96 + k * 32]
        send(("s", d), pf.at[d, 1 - c], sib.at[d], sibling)
    for d in (2, 1, 3):
        got("s", d)
        ysend[d - 1] = (pf[d, c] + sib[d]).astype(BF16)
        send(("y", d), ysend.at[d - 1], yr.at[d - 1], device(x, y + d, z, c))
    got("s", 0)
    ysum[...] = pf[0, c] + sib[0]

    def grads(zi):
        g = zlab[zi]
        w = wk[pl.ds(g * 4, 4)].reshape(512, 1024)
        block = lax.dot_general(
            cots[...].reshape(512, 1024), w, (((1,), (1,)), ((), ())), preferred_element_type=F32
        ).astype(BF16)
        orecv[q, g] = block[0:128]
        for k in range(1, 4):
            osend[k - 1, zi] = block[k * 128 : k * 128 + 128]
        send(("o", 1, zi), osend.at[1, zi], orecv.at[q, g], behind_same)
        send(("o", 2, zi), osend.at[2, zi], orecv.at[q, g], ahead_other)
        send(("o", 0, zi), osend.at[0, zi], orecv.at[q, g], sibling)

    for at in range(7 - LAG, 6):
        level(1, at)
    grads(0)
    grads(1)

    for d in (1, 3, 2):
        got("y", d)
        ysum[...] += yr[d - 1].astype(F32)
    for k in (4, 3, 5, 2, 6, 1, 7):
        zt = (z + k) % 8
        rows = pl.ds(pl.multiple_of((zt % 2) * 32 + (zt // 2) * 8, 8), 8)
        send(("z", k), ysum.at[rows], zr.at[k - 1], device(x, y, z + k, c))
    grads(2)
    total = ysum[pl.ds(pl.multiple_of(zl * 32 + zh * 8, 8), 8), :]
    for k in range(1, 8):
        got("z", k)
        total += zr[k - 1]
    xx[x] = total
    for k in (2, 1, 3):
        send(("x", k), xx.at[x], xx.at[x], device(x + k, y, z, c))
    level(1, 6)
    grads(3)
    for k in (1, 2, 3):
        got("x", k)
        got("m", 0, k)
        got("m", 1, k)
    grad = (xx[0] + xx[1]) + (xx[2] + xx[3])
    moment_first = jnp.concatenate([mom[0, k] for k in range(4)], axis=0)
    moment_second = jnp.concatenate([mom[1, k] for k in range(4)], axis=0)
    first = 0.9 * moment_first + 0.1 * grad
    second = 0.999 * moment_second + 0.001 * grad * grad
    mean_hat = first / (1.0 - 0.9**STEP)
    var_hat = second / (1.0 - 0.999**STEP)
    direction = mean_hat / (jnp.sqrt(var_hat) + 1e-08)
    dz[z] = jnp.concatenate([direction[:, 0:512], direction[:, 512:1024]], axis=0).astype(BF16)
    for k in (4, 3, 5, 2, 6, 1, 7):
        send(("dz", k), dz.at[z], dz.at[z], device(x, y, z + k, c))

    def own(rows):
        picked = rows[0:2]
        for k in range(1, 4):
            picked = jnp.where(x == k, rows[2 * k : 2 * k + 2], picked)
        return picked

    pg_ref[...] = own(grad)
    first_ref[...] = own(first)
    second_ref[...] = own(second)

    for k in range(1, 8):
        got("dz", k)
    for k in range(8):
        block = dz[k].astype(F32)
        row = (k % 2) * 32 + (k // 2) * 8
        d64[row : row + 8, 0:512] = block[0:8]
        d64[row : row + 8, 512:1024] = block[8:16]
    dall[y, c] = d64[...].astype(BF16)
    for k in (2, 1, 3):
        send(("dy", k), dall.at[y, c], dall.at[y, c], device(x, y + k, z, c))
    send(("ds", 0), dall.at[y, c], dall.at[y, c], sibling)

    for zi in range(4):
        for k in range(3):
            got("o", k, zi)
    for k in range(4):
        for s in range(16):
            out_ref[:, s * 512 + k * 128 : s * 512 + k * 128 + 128] = orecv[
                k, s // 4, :, (s % 4) * 128 : (s % 4) * 128 + 128
            ]

    for k in (1, 3, 2):
        got("dy", k)
        block = dall.at[(y + 4 - k) % 4, c]
        send(("ds", k), block, block, sibling)
    for k in (0, 1, 3, 2):
        got("ds", k)
    rows = [dall[i, k, zz * 32 : zz * 32 + 32] for i in range(4) for zz in range(2) for k in range(2)]
    fu_ref[...] = jnp.dot(
        basis_ref[...], jnp.concatenate(rows, axis=0), preferred_element_type=F32
    ).astype(BF16)

    for copy in copies.values():
        copy.wait_send()


COPIES = 160


def on_device(inputs, cotangent, kv_weight, basis, moment_first, moment_second):
    vmem = pl.BlockSpec(memory_space=pltpu.VMEM)
    shape = jax.ShapeDtypeStruct
    return pl.pallas_call(
        kernel,
        out_shape=(
            shape((128, 8192), BF16),
            shape((512, 1024), BF16),
            shape((2, 1024), F32),
            shape((2, 1024), F32),
            shape((2, 1024), F32),
        ),
        in_specs=[vmem] * 6,
        out_specs=[vmem] * 5,
        scratch_shapes=[
            pltpu.VMEM((4, 128, 2048), BF16),
            pltpu.VMEM((4, 128, 2048), BF16),
            pltpu.VMEM((4, 128, 1024), BF16),
            pltpu.VMEM((16, 128, 512), BF16),
            pltpu.VMEM((16, 128, 1024), BF16),
            pltpu.VMEM((2, 4, 2, 1024), F32),
            pltpu.VMEM((512, 512), BF16),
            pltpu.VMEM((4, 2, 64, 1024), F32),
            pltpu.VMEM((4, 64, 1024), F32),
            pltpu.VMEM((64, 1024), F32),
            pltpu.VMEM((3, 64, 1024), BF16),
            pltpu.VMEM((3, 64, 1024), BF16),
            pltpu.VMEM((7, 8, 1024), F32),
            pltpu.VMEM((4, 8, 1024), F32),
            pltpu.VMEM((8, 16, 512), BF16),
            pltpu.VMEM((64, 1024), F32),
            pltpu.VMEM((4, 2, 64, 1024), BF16),
            pltpu.VMEM((3, 4, 128, 512), BF16),
            pltpu.VMEM((4, 4, 128, 512), BF16),
            pltpu.SemaphoreType.DMA((COPIES,)),
            pltpu.SemaphoreType.DMA((COPIES,)),
        ],
        compiler_params=pltpu.CompilerParams(
            collective_id=0, has_side_effects=True, vmem_limit_bytes=48 << 20
        ),
    )(inputs, cotangent, kv_weight, basis, moment_first, moment_second)


def solution(mesh):
    tokens = P(("rep", "dp"), None)
    shard = P("dp", None)
    return jax.shard_map(
        on_device,
        mesh=mesh,
        in_specs=(tokens, tokens, shard, shard, tokens, tokens),
        out_specs=(tokens, shard, tokens, tokens, tokens),
        check_vma=False,
    )
```

```python
import functools

import jax
import jax.numpy as jnp
from jax import lax
from jax.experimental import pallas as pl
from jax.experimental.pallas import tpu as pltpu
from jax.sharding import PartitionSpec as P

MESH = pl.DeviceIdType.MESH
STEP = 20
TOKENS = 32768
F32 = jnp.float32
BF16 = jnp.bfloat16
SCALE = float(TOKENS) ** -0.5
SCHEDULE = (
    ("z", 0, 0, 0, 1), ("x", 0, 64, 0, 1, 0), ("x", 0, 64, 0, 1, 1), ("x", 0, 0, 0, 1, 0),
    ("z", 0, 64, 0, 1), ("tok",), ("x", 0, 0, 0, 1, 1), ("z", 1, 0, 0, 1), ("x", 1, 64, 0, 1, 0),
    ("x", 1, 64, 0, 1, 1), ("z", 0, 0, 0, 2), ("x", 0, 64, 0, 2, 0), ("x", 0, 64, 0, 2, 1),
    ("z", 0, 64, 1, 1), ("z", 0, 64, 2, 1), ("x", 0, 0, 1, 1, 0), ("x", 0, 0, 1, 1, 1), ("sw",),
    ("z", 0, 64, 0, 2), ("x", 0, 0, 0, 2, 1), ("x", 0, 0, 0, 2, 0), ("mo",), ("cf",), ("z", 0, 0, 0, 3),
    ("x", 0, 0, 2, 1, 1), ("x", 0, 0, 2, 1, 0), ("z", 1, 0, 0, 2), ("x", 0, 64, 0, 3, 0),
    ("x", 0, 64, 0, 3, 1), ("z", 0, 64, 3, 1), ("z", 0, 64, 1, 2), ("z", 0, 64, 0, 3), ("x", 1, 64, 0, 2, 0),
    ("x", 1, 64, 0, 2, 1), ("x", 0, 0, 1, 2, 0), ("x", 0, 0, 1, 2, 1), ("z", 0, 64, 2, 2),
    ("x", 0, 0, 0, 3, 0), ("x", 0, 0, 0, 3, 1), ("z", 0, 0, 0, 4), ("x", 1, 0, 0, 1, 0),
    ("x", 1, 0, 1, 1, 1), ("z", 1, 64, 0, 1), ("x", 0, 0, 2, 2, 0), ("x", 0, 0, 2, 2, 1), ("z", 0, 0, 0, 5),
    ("x", 0, 0, 3, 1, 0), ("x", 0, 0, 3, 1, 1), ("z", 0, 64, 3, 2), ("x", 1, 64, 0, 3, 0),
    ("x", 1, 64, 0, 3, 1), ("z", 0, 64, 0, 4), ("x", 0, 0, 1, 3, 0), ("x", 0, 0, 1, 3, 1),
    ("z", 0, 64, 1, 3), ("z", 0, 64, 0, 5), ("z", 0, 64, 2, 3), ("x", 1, 0, 1, 1, 0), ("x", 1, 0, 0, 1, 1),
    ("z", 1, 64, 0, 2), ("z", 0, 64, 3, 3), ("x", 0, 0, 2, 3, 0), ("x", 0, 0, 2, 3, 1), ("pa",),
    ("x", 0, 0, 3, 2, 0), ("x", 0, 0, 3, 2, 1), ("z", 0, 64, 2, 4), ("z", 0, 64, 1, 4), ("z", 0, 64, 1, 5),
    ("z", 1, 64, 3, 1), ("x", 1, 0, 0, 2, 0), ("x", 1, 0, 1, 2, 1), ("z", 0, 64, 2, 5), ("z", 0, 64, 3, 4),
    ("x", 1, 0, 1, 2, 0), ("x", 1, 0, 0, 2, 1), ("z", 0, 64, 3, 5), ("z", 1, 64, 1, 1), ("x", 0, 0, 3, 3, 0),
    ("x", 0, 0, 3, 3, 1), ("pj",), ("pp", 2), ("pp", 1), ("pp", 3), ("pp", 0), ("as", 2), ("as", 1),
    ("z", 1, 64, 2, 1), ("z", 1, 64, 3, 2), ("as", 3), ("x", 1, 0, 0, 3, 1), ("x", 1, 0, 1, 3, 1),
    ("x", 1, 0, 0, 3, 0), ("as", 0), ("o", 0), ("z", 1, 0, 0, 3), ("z", 1, 64, 1, 2), ("x", 1, 0, 2, 1, 1),
    ("x", 1, 0, 2, 1, 0), ("x", 1, 0, 1, 3, 0), ("z", 1, 64, 0, 3), ("ay",), ("z", 1, 64, 2, 2),
    ("z", 1, 64, 3, 3), ("o", 1), ("z", 1, 64, 1, 3), ("x", 1, 0, 2, 2, 0), ("x", 1, 0, 2, 2, 1),
    ("z", 1, 0, 0, 4), ("z", 1, 64, 3, 4), ("az",), ("z", 1, 64, 2, 3), ("z", 1, 64, 1, 4),
    ("x", 1, 0, 2, 3, 0), ("x", 1, 0, 2, 3, 1), ("o", 2), ("z", 1, 0, 0, 5), ("x", 1, 0, 3, 1, 0),
    ("z", 1, 64, 0, 4), ("x", 1, 0, 3, 1, 1), ("z", 1, 64, 3, 5), ("ad",), ("z", 1, 64, 1, 5),
    ("z", 1, 64, 2, 4), ("z", 1, 64, 0, 5), ("x", 1, 0, 3, 2, 0), ("x", 1, 0, 3, 2, 1), ("z", 1, 64, 2, 5),
    ("gz",), ("x", 1, 0, 3, 3, 0), ("x", 1, 0, 3, 3, 1), ("o", 3), ("gy",), ("up",), ("co",),
)


def device(x, y, z, c):
    return ((y % 4) * 4 + (z % 2) * 2 + c, ((z % 8) // 2) * 4 + x % 4)


def kernel(
    x_hbm, cot_hbm, kv_hbm, basis_hbm, m1_hbm, m2_hbm,
    out_ref, fu_ref, pg_ref,
    x_ref, basis_ref, basis_swapped, swap, swapped, proj, acc, xq, xr, cots, wb, wk, mom, pt, pf, sib, ysum, ysend, yr, zsend, zr, xx, dz, d64, dall, osend, orecv,
    load_sem, send_sem, recv_sem,
):
    rep, dp = lax.axis_index("rep"), lax.axis_index("dp")
    c, zl, y = rep % 2, (rep // 2) % 2, rep // 4
    zh, x = dp // 4, dp % 4
    z = zh * 2 + zl
    e = y % 2
    q = e * 2 + c
    dy = 1 - 2 * c + 4
    sigma = 2 * zl - 1 + 4
    half = 1 - zl
    zlab = [zh, (zh + sigma) % 4, (zh + 8 - sigma) % 4, (zh + 2) % 4]
    xlab = [x, (x + 3) % 4, (x + 1) % 4, (x + 2) % 4]
    outer = device(x, y, z + 8 + 2 * zl - 1, c)
    inner = device(x, y, z + 1 - 2 * zl, c)
    outer_far = device(x, y, z + 8 + 4 * zl - 2, c)
    right, left = device(x + 1, y, z, c), device(x + 3, y, z, c)
    sibling = device(x, y, z, 1 - c)
    left_half, right_half = slice(0, 512), slice(512, 1024)
    ahead_same = device(x, y + dy, z, c)
    ahead_other = device(x, y + dy, z, 1 - c)
    behind_same = device(x, y + 8 - dy, z, c)
    behind_other = device(x, y + 8 - dy, z, 1 - c)

    barrier = pltpu.get_barrier_semaphore()
    friends = [sibling, ahead_same, ahead_other, behind_same, behind_other, device(x, y + 2, z, c)]
    friends += [right, left, outer, inner]
    for friend in friends:
        pl.semaphore_signal(barrier, inc=1, device_id=friend, device_id_type=MESH)

    mine = zh * 4 + x
    quarter = pl.ds(pl.multiple_of(q * 128, 128), 128)
    loads = [
        pltpu.make_async_copy(src, dst, load_sem.at[k])
        for k, (src, dst) in enumerate((
            (basis_hbm.at[quarter], wb.at[mine]),
            (cot_hbm, cots.at[0]),
            (x_hbm, x_ref),
            (kv_hbm.at[quarter], wk.at[mine]),
            (m1_hbm.at[:, pl.ds(0, 512)], mom.at[0, 0, x]),
            (m1_hbm.at[:, pl.ds(512, 512)], mom.at[1, 0, y]),
            (m2_hbm.at[:, pl.ds(0, 512)], mom.at[0, 1, x]),
            (m2_hbm.at[:, pl.ds(512, 512)], mom.at[1, 1, y]),
            (basis_hbm, basis_ref),
        ))
    ]
    for load in loads:
        load.start()
    for load in loads[:2]:
        load.wait()
    pl.semaphore_wait(barrier, len(friends))

    copies = {}

    def send(name, src, dst, target):
        k = len(copies)
        copy = pltpu.make_async_remote_copy(
            src_ref=src, dst_ref=dst, send_sem=send_sem.at[k], recv_sem=recv_sem.at[k],
            device_id=target, device_id_type=MESH,
        )
        copy.start()
        copies[name] = copy

    def got(*name):
        copies[name].wait_recv()

    weights = (wb, wk)

    def piece(w, zi, xi, row, rows):
        return weights[w].at[zlab[zi] * 4 + xlab[xi], pl.ds(row, rows)]

    def push(name, w, zi, xi, row, rows, target):
        ref = piece(w, zi, xi, row, rows)
        send(name, ref, ref, target)

    def z_step(w, base, xi, step):
        n = (w, base, xi)
        lower = pl.multiple_of(base + 32 * half, 32)
        upper = pl.multiple_of(base + 32 - 32 * half, 32)
        if step == 1:
            push(n + ("z1",), w, 0, xi, base, 64, outer)
        elif step == 2:
            got(*n, "z1")
            push(n + ("z2",), w, 1, xi, base, 64, inner)
        elif step == 3:
            got(*n, "z2")
            push(n + ("z3",), w, 2, xi, lower, 32, outer)
            if w == 0:
                push(n + ("z4",), w, 2, xi, lower, 32, outer_far)
        elif step == 4:
            got(*n, "z3")
            if w == 1:
                push(n + ("z4",), w, 3, xi, upper, 32, inner)
        else:
            got(*n, "z4")

    def x_step(w, base, zi, step, side):
        n = (w, base, zi, side)
        target = (right, left)[side]
        if step == 1:
            push(n + ("full",), w, zi, 0, base, 64, target)
        elif step == 2:
            got(*n, "full")
            push(n + ("half",), w, zi, 1 + side, base + 32 * side, 32, target)
        else:
            got(*n, "half")

    def share_tokens():
        send("c_near", cots.at[0], cots.at[2], ahead_same)
        loads[2].wait()
        for k in range(4):
            for s in range(16):
                xq[k, :, s * 128 : s * 128 + 128] = x_ref[:, s * 512 + k * 128 : s * 512 + k * 128 + 128]
        other = 2 - 2 * e
        send("x_near", xq.at[other + c], xr.at[2], ahead_same)
        send("x_cross", xq.at[other + 1 - c], xr.at[3], ahead_other)
        send("x_sib", xq.at[e * 2 + 1 - c], xr.at[1], sibling)
        send("c_sib", cots.at[0], cots.at[1], sibling)
        for load in loads[3:]:
            load.wait()

    def share_moments():
        for k in (1, 2, 3):
            for j in range(2):
                ref = mom.at[0, j, x]
                send(("m", 0, j, k), ref, ref, device(x + k, y, z, c))
                ref = mom.at[1, j, y]
                send(("m", 1, j, k), ref, ref, device(x, y + k, z, c))

    def forward_cotangent():
        copies["c_near"].wait_recv()
        send("c_cross", cots.at[2], cots.at[3], sibling)

    def project_group(zi):
        g = zlab[zi]
        columns = pl.ds(pl.multiple_of(g * 512, 512), 512)
        w = wb[pl.ds(g * 4, 4)].reshape(512, 512)
        return jnp.dot(xr[:, :, columns].reshape(512, 512), w, preferred_element_type=F32)

    def project_early():
        xr[0] = xq[q]
        for name in ("x_sib", "x_near", "x_cross"):
            copies[name].wait_recv()
        proj[...] = (project_group(0) + project_group(1)) + project_group(2)

    def project():
        pt[...] = (proj[...] + project_group(3)).T.astype(BF16)
        swapped[...] = jnp.dot(swap[...], pt[...], preferred_element_type=F32).astype(BF16)

    def prepare_swap():
        row = lax.broadcasted_iota(jnp.int32, (512, 512), 0)
        column = lax.broadcasted_iota(jnp.int32, (512, 512), 1)
        low, high = (row >> 1) & 3, row >> 7
        other_row = row + (low - high) * 126
        swap[...] = jnp.where(column == other_row, 1.0, 0.0).astype(BF16)
        basis_swapped[...] = jnp.dot(basis_ref[...], swap[...], preferred_element_type=F32).astype(BF16)

    def products(d):
        if d == 2:
            for name in ("c_sib", "c_cross"):
                copies[name].wait_recv()
        for at, matrix, columns in ((y, pt, left_half), (x, swapped, right_half)):
            rows = pl.ds(pl.multiple_of(((at + d) % 4) * 128, 128), 128)
            cot = cots[:, :, columns].reshape(512, 512)
            block = jnp.dot(matrix[rows, :], cot, preferred_element_type=F32)
            for k in range(2):
                pf[d, k, 0:32, columns] = block[k * 32 : k * 32 + 32]
                pf[d, k, 32:64, columns] = block[64 + k * 32 : 96 + k * 32]
        send(("s", d), pf.at[d, 1 - c], sib.at[d], sibling)

    def add_sibling(d):
        got("s", d)
        both = pf[d, c] + sib[d]
        if d == 0:
            ysum[...] = both
            return
        ysend[0, d - 1] = both[:, left_half].astype(BF16)
        ysend[1, d - 1] = both[:, right_half].astype(BF16)
        send(("y", 0, d), ysend.at[0, d - 1], yr.at[0, d - 1], device(x, y + d, z, c))
        send(("y", 1, d), ysend.at[1, d - 1], yr.at[1, d - 1], device(x + d, y, z, c))

    def grads(zi):
        g = zlab[zi]
        w = wk[pl.ds(g * 4, 4)].reshape(512, 1024)
        block = lax.dot_general(
            cots[...].reshape(512, 1024), w, (((1,), (1,)), ((), ())), preferred_element_type=F32
        ).astype(BF16)
        orecv[q, g] = block[0:128]
        for k in range(1, 4):
            osend[k - 1, zi] = block[k * 128 : k * 128 + 128]
        send(("o", 1, zi), osend.at[1, zi], orecv.at[q, g], behind_same)
        send(("o", 2, zi), osend.at[2, zi], orecv.at[q, g], ahead_other)
        send(("o", 0, zi), osend.at[0, zi], orecv.at[q, g], sibling)

    def add_y():
        for d in (1, 3, 2):
            got("y", 0, d)
            got("y", 1, d)
            ysum[...] += jnp.concatenate([yr[0, d - 1], yr[1, d - 1]], axis=1).astype(F32)
        for k in (4, 3, 5, 2, 6, 1, 7):
            zt = (z + k) % 8
            rows = ysum[pl.ds(pl.multiple_of((zt % 2) * 32 + (zt // 2) * 8, 8), 8), :]
            zsend[k - 1] = jnp.concatenate([rows[:, left_half], rows[:, right_half]], axis=0).astype(BF16)
            send(("z", k), zsend.at[k - 1], zr.at[k - 1], device(x, y, z + k, c))

    def add_z():
        total = ysum[pl.ds(pl.multiple_of(zl * 32 + zh * 8, 8), 8), :]
        for k in (1, 7, 2, 6, 3, 5, 4):
            got("z", k)
            rows = zr[k - 1].astype(F32)
            total += jnp.concatenate([rows[0:8], rows[8:16]], axis=1)
        xx[0, x] = total[:, left_half]
        xx[1, y] = total[:, right_half]
        for k in (2, 1, 3):
            send(("x", 0, k), xx.at[0, x], xx.at[0, x], device(x + k, y, z, c))
            send(("x", 1, k), xx.at[1, y], xx.at[1, y], device(x, y + k, z, c))

    def adam():
        for k in (1, 3, 2):
            for h in range(2):
                got("m", h, 0, k)
                got("m", h, 1, k)
                got("x", h, k)
        raw = jnp.concatenate([(xx[h, 0] + xx[h, 1]) + (xx[h, 2] + xx[h, 3]) for h in range(2)], axis=1)
        grad = SCALE * raw
        moment_first, moment_second = (
            jnp.concatenate(
                [jnp.concatenate([mom[h, j, k] for k in range(4)], axis=0) for h in range(2)], axis=1
            )
            for j in range(2)
        )
        first = 0.9 * moment_first + 0.1 * grad
        second = 0.999 * moment_second + 0.001 * grad * grad
        mean_hat = first / (1.0 - 0.9**STEP)
        var_hat = second / (1.0 - 0.999**STEP)
        direction = mean_hat / (jnp.sqrt(var_hat) + 1e-08)
        dz[z] = jnp.concatenate([direction[:, 0:512], direction[:, 512:1024]], axis=0).astype(BF16)
        for k in (4, 3, 5, 2, 6, 1, 7):
            send(("dz", k), dz.at[z], dz.at[z], device(x, y, z + k, c))
        for at, columns in ((x, left_half), (y, right_half)):
            picked = raw[0:2, columns]
            for k in range(1, 4):
                picked = jnp.where(at == k, raw[2 * k : 2 * k + 2, columns], picked)
            pg_ref[:, columns] = picked

    def gather_z():
        for k in (1, 7, 2, 6, 3, 5, 4):
            got("dz", k)
        for k in range(8):
            block = dz[k].astype(F32)
            row = (k % 2) * 32 + (k // 2) * 8
            d64[row : row + 8, 0:512] = block[0:8]
            d64[row : row + 8, 512:1024] = block[8:16]
        both = d64[...].astype(BF16)
        dall[0, y, c] = both[:, left_half]
        dall[1, x, c] = both[:, right_half]
        mine_left, mine_right = dall.at[0, y, c], dall.at[1, x, c]
        for k in (2, 1, 3):
            send(("dy", 0, k), mine_left, mine_left, device(x, y + k, z, c))
            send(("dy", 1, k), mine_right, mine_right, device(x + k, y, z, c))
        send(("ds", 0, 0), mine_left, mine_left, sibling)
        send(("ds", 1, 0), mine_right, mine_right, sibling)

    def collect():
        for zi in range(4):
            for k in range(3):
                got("o", k, zi)
        for k in range(4):
            for s in range(16):
                out_ref[:, s * 512 + k * 128 : s * 512 + k * 128 + 128] = orecv[
                    k, s // 4, :, (s % 4) * 128 : (s % 4) * 128 + 128
                ]

    def update_part(shifts):
        products = []
        for h, (at, matrix) in enumerate(((y, basis_ref), (x, basis_swapped))):
            parts = [(at + k) % 4 for k in shifts]
            rows = [dall[h, i, k, zz * 32 : zz * 32 + 32] for i in parts for zz in range(2) for k in range(2)]
            columns = [matrix[:, pl.ds(pl.multiple_of(i * 128, 128), 128)] for i in parts]
            products.append(jnp.dot(
                jnp.concatenate(columns, axis=1), jnp.concatenate(rows, axis=0), preferred_element_type=F32
            ))
        return jnp.concatenate(products, axis=1)

    def forward_rows(k):
        for h, at in ((0, y), (1, x)):
            got("dy", h, k)
            block = dall.at[h, (at + 4 - k) % 4, c]
            send(("ds", h, k), block, block, sibling)

    def got_rows(k):
        got("ds", 0, k)
        got("ds", 1, k)

    def gather_y():
        forward_rows(1)
        forward_rows(3)
        for k in (0, 1, 3):
            got_rows(k)
        acc[...] = update_part([0, 3, 1])

    def update():
        forward_rows(2)
        got_rows(2)
        fu_ref[...] = (acc[...] + update_part([2])).astype(BF16)

    stages = {
        "z": z_step, "x": x_step, "o": grads, "tok": share_tokens,
        "cf": forward_cotangent, "mo": share_moments, "sw": prepare_swap, "pa": project_early, "pj": project, "pp": products, "as": add_sibling, "ay": add_y,
        "az": add_z, "ad": adam, "gz": gather_z, "co": collect, "gy": gather_y, "up": update,
    }
    for word, *where in SCHEDULE:
        stages[word](*where)

    for copy in copies.values():
        copy.wait_send()


COPIES = 176


def on_device(inputs, cotangent, kv_weight, basis, moment_first, moment_second):
    vmem = pl.BlockSpec(memory_space=pltpu.VMEM)
    shape = jax.ShapeDtypeStruct
    hbm = pl.BlockSpec(memory_space=pltpu.HBM)
    operands = [
        pltpu.with_memory_space_constraint(a, pltpu.HBM)
        for a in (inputs, cotangent, kv_weight, basis, moment_first, moment_second)
    ]
    input_grad, full_update, raw = pl.pallas_call(
        kernel,
        out_shape=(
            shape((128, 8192), BF16),
            shape((512, 1024), BF16),
            shape((2, 1024), F32),
        ),
        in_specs=[hbm] * 6,
        out_specs=[vmem] * 3,
        scratch_shapes=[
            pltpu.VMEM((128, 8192), BF16),
            pltpu.VMEM((512, 512), BF16),
            pltpu.VMEM((512, 512), BF16),
            pltpu.VMEM((512, 512), BF16),
            pltpu.VMEM((512, 512), BF16),
            pltpu.VMEM((512, 512), F32),
            pltpu.VMEM((512, 1024), F32),
            pltpu.VMEM((4, 128, 2048), BF16),
            pltpu.VMEM((4, 128, 2048), BF16),
            pltpu.VMEM((4, 128, 1024), BF16),
            pltpu.VMEM((16, 128, 512), BF16),
            pltpu.VMEM((16, 128, 1024), BF16),
            pltpu.VMEM((2, 2, 4, 2, 512), F32),
            pltpu.VMEM((512, 512), BF16),
            pltpu.VMEM((4, 2, 64, 1024), F32),
            pltpu.VMEM((4, 64, 1024), F32),
            pltpu.VMEM((64, 1024), F32),
            pltpu.VMEM((2, 3, 64, 512), BF16),
            pltpu.VMEM((2, 3, 64, 512), BF16),
            pltpu.VMEM((7, 16, 512), BF16),
            pltpu.VMEM((7, 16, 512), BF16),
            pltpu.VMEM((2, 4, 8, 512), F32),
            pltpu.VMEM((8, 16, 512), BF16),
            pltpu.VMEM((64, 1024), F32),
            pltpu.VMEM((2, 4, 2, 64, 512), BF16),
            pltpu.VMEM((3, 4, 128, 512), BF16),
            pltpu.VMEM((4, 4, 128, 512), BF16),
            pltpu.SemaphoreType.DMA((9,)),
            pltpu.SemaphoreType.DMA((COPIES,)),
            pltpu.SemaphoreType.DMA((COPIES,)),
        ],
        compiler_params=pltpu.CompilerParams(
            collective_id=0, has_side_effects=True, vmem_limit_bytes=48 << 20
        ),
    )(*operands)
    proj_grad = SCALE * raw
    first_new = 0.9 * moment_first + 0.1 * proj_grad
    second_new = 0.999 * moment_second + 0.001 * proj_grad * proj_grad
    return input_grad, full_update, proj_grad, first_new, second_new


def solution(mesh):
    tokens = P(("rep", "dp"), None)
    shard = P("dp", None)
    return jax.shard_map(
        on_device,
        mesh=mesh,
        in_specs=(tokens, tokens, shard, shard, tokens, tokens),
        out_specs=(tokens, shard, tokens, tokens, tokens),
        check_vma=False,
    )
```

```python
import functools

import jax
import jax.numpy as jnp
from jax import lax
from jax.experimental import pallas as pl
from jax.experimental.pallas import tpu as pltpu
from jax.sharding import PartitionSpec as P

MESH = pl.DeviceIdType.MESH
STEP = 20
TOKENS = 32768
F32 = jnp.float32
BF16 = jnp.bfloat16
SCALE = float(TOKENS) ** -0.5
SCHEDULE = (
    ("z", 0, 0, 0, 1), ("x", 0, 64, 0, 1, 1), ("x", 0, 64, 0, 1, 0), ("tok",), ("x", 0, 0, 0, 1, 1),
    ("x", 0, 0, 0, 1, 0), ("z", 0, 64, 0, 1), ("z", 0, 0, 0, 2), ("x", 0, 64, 0, 2, 1),
    ("x", 0, 64, 0, 2, 0), ("z", 0, 64, 2, 1), ("x", 0, 0, 1, 1, 0), ("z", 0, 64, 1, 1),
    ("x", 0, 0, 1, 1, 1), ("sw",), ("x", 0, 0, 0, 2, 1), ("z", 0, 64, 0, 2), ("x", 0, 0, 0, 2, 0),
    ("x", 0, 64, 0, 3, 1), ("x", 0, 64, 0, 3, 0), ("z", 0, 64, 3, 1), ("z", 0, 0, 0, 3),
    ("x", 0, 0, 2, 1, 0), ("x", 0, 0, 2, 1, 1), ("z", 0, 64, 2, 2), ("x", 0, 0, 1, 2, 0),
    ("x", 0, 0, 1, 2, 1), ("x", 0, 0, 0, 3, 1), ("z", 0, 64, 1, 2), ("x", 0, 0, 0, 3, 0), ("z", 0, 64, 0, 3),
    ("z", 0, 64, 3, 2), ("x", 0, 0, 2, 2, 0), ("x", 0, 0, 2, 2, 1), ("z", 0, 64, 2, 3), ("x", 0, 0, 1, 3, 0),
    ("z", 0, 0, 0, 4), ("x", 0, 0, 1, 3, 1), ("z", 0, 0, 0, 5), ("x", 0, 0, 3, 1, 0), ("z", 0, 64, 1, 3),
    ("x", 0, 0, 3, 1, 1), ("z", 0, 64, 0, 4), ("x", 1, 64, 0, 1, 0), ("z", 1, 64, 0, 1), ("z", 0, 64, 0, 5),
    ("x", 1, 64, 0, 1, 1), ("x", 0, 0, 2, 3, 0), ("z", 0, 64, 3, 3), ("x", 0, 0, 2, 3, 1), ("pa",),
    ("z", 0, 64, 1, 4), ("z", 0, 64, 2, 4), ("cf",), ("x", 0, 0, 3, 2, 0), ("x", 0, 0, 3, 2, 1),
    ("z", 0, 64, 2, 5), ("mo",), ("z", 0, 64, 1, 5), ("z", 1, 0, 0, 1), ("x", 1, 0, 0, 1, 1),
    ("x", 1, 0, 0, 1, 0), ("z", 1, 64, 0, 2), ("x", 0, 0, 3, 3, 0), ("z", 0, 64, 3, 4), ("x", 0, 0, 3, 3, 1),
    ("x", 1, 64, 0, 2, 1), ("x", 1, 64, 0, 2, 0), ("z", 1, 64, 2, 1), ("z", 0, 64, 3, 5), ("pj",), ("pp", 2),
    ("pp", 1), ("pp", 3), ("pp", 0), ("as", 2), ("as", 1), ("x", 1, 64, 0, 3, 1), ("z", 1, 0, 0, 2),
    ("as", 3), ("x", 1, 64, 0, 3, 0), ("z", 1, 64, 1, 1), ("as", 0), ("x", 1, 0, 1, 1, 1),
    ("x", 1, 0, 1, 1, 0), ("z", 1, 64, 2, 2), ("z", 1, 64, 3, 1), ("x", 1, 0, 0, 2, 1), ("x", 1, 0, 0, 2, 0),
    ("ay",), ("z", 1, 0, 0, 3), ("x", 1, 0, 2, 1, 1), ("x", 1, 0, 2, 1, 0), ("z", 1, 64, 1, 2),
    ("z", 1, 64, 0, 3), ("x", 1, 0, 0, 3, 0), ("x", 1, 0, 0, 3, 1), ("o", 0), ("x", 1, 0, 1, 2, 1),
    ("x", 1, 0, 1, 2, 0), ("z", 1, 64, 2, 3), ("z", 1, 0, 0, 4), ("az",), ("z", 1, 64, 3, 2),
    ("x", 1, 0, 2, 2, 1), ("x", 1, 0, 2, 2, 0), ("z", 1, 64, 1, 3), ("x", 1, 0, 1, 3, 1),
    ("x", 1, 0, 1, 3, 0), ("o", 1), ("z", 1, 0, 0, 5), ("x", 1, 0, 3, 1, 0), ("x", 1, 0, 3, 1, 1), ("ad",),
    ("co", 0), ("x", 1, 0, 2, 3, 1), ("x", 1, 0, 2, 3, 0), ("z", 1, 64, 1, 4), ("z", 1, 64, 3, 3), ("o", 2),
    ("z", 1, 64, 0, 4), ("z", 1, 64, 2, 4), ("co", 1), ("x", 1, 0, 3, 2, 0), ("x", 1, 0, 3, 2, 1),
    ("z", 1, 64, 1, 5), ("z", 1, 64, 3, 4), ("gz",), ("z", 1, 64, 0, 5), ("co", 2), ("z", 1, 64, 2, 5),
    ("x", 1, 0, 3, 3, 0), ("x", 1, 0, 3, 3, 1), ("z", 1, 64, 3, 5), ("o", 3), ("gy",), ("up",), ("co", 3),
)
SETTLE = ("as", "ay", "az", "ad", "gz")


def device(x, y, z, c):
    return ((y % 4) * 4 + (z % 2) * 2 + c, ((z % 8) // 2) * 4 + x % 4)


def kernel(
    x_hbm, cot_hbm, kv_hbm, basis_hbm, m1_hbm, m2_hbm,
    out_ref, fu_ref, pg_ref,
    x_ref, basis_ref, basis_swapped, swap, swapped, proj, acc, xq, xr, cots, wb, wk, mom, pt, pf, sib, ysum, ysend, yr, zsend, zr, xx, dz, d64, dall, osend, orecv,
    load_sem, send_sem, recv_sem,
):
    rep, dp = lax.axis_index("rep"), lax.axis_index("dp")
    c, zl, y = rep % 2, (rep // 2) % 2, rep // 4
    zh, x = dp // 4, dp % 4
    z = zh * 2 + zl
    e = y % 2
    q = e * 2 + c
    dy = 1 - 2 * c + 4
    sigma = 2 * zl - 1 + 4
    half = 1 - zl
    zlab = [zh, (zh + sigma) % 4, (zh + 8 - sigma) % 4, (zh + 2) % 4]
    xlab = [x, (x + 3) % 4, (x + 1) % 4, (x + 2) % 4]
    outer = device(x, y, z + 8 + 2 * zl - 1, c)
    inner = device(x, y, z + 1 - 2 * zl, c)
    outer_far = device(x, y, z + 8 + 4 * zl - 2, c)
    right, left = device(x + 1, y, z, c), device(x + 3, y, z, c)
    sibling = device(x, y, z, 1 - c)
    left_half, right_half = slice(0, 512), slice(512, 1024)
    ahead_same = device(x, y + dy, z, c)
    ahead_other = device(x, y + dy, z, 1 - c)
    behind_same = device(x, y + 8 - dy, z, c)
    behind_other = device(x, y + 8 - dy, z, 1 - c)

    barrier = pltpu.get_barrier_semaphore()
    friends = [sibling, ahead_same, ahead_other, behind_same, behind_other]
    friends += [right, left, outer, inner]
    for friend in friends:
        pl.semaphore_signal(barrier, inc=1, device_id=friend, device_id_type=MESH)

    mine = zh * 4 + x
    quarter = pl.ds(pl.multiple_of(q * 128, 128), 128)
    loads = [
        pltpu.make_async_copy(src, dst, load_sem.at[k])
        for k, (src, dst) in enumerate((
            (basis_hbm.at[quarter], wb.at[mine]),
            (cot_hbm, cots.at[0]),
            (x_hbm, x_ref),
            (kv_hbm.at[quarter], wk.at[mine]),
            (m1_hbm.at[:, pl.ds(0, 512)], mom.at[0, 0, x]),
            (m1_hbm.at[:, pl.ds(512, 512)], mom.at[1, 0, y]),
            (m2_hbm.at[:, pl.ds(0, 512)], mom.at[0, 1, x]),
            (m2_hbm.at[:, pl.ds(512, 512)], mom.at[1, 1, y]),
            (basis_hbm, basis_ref),
        ))
    ]
    for load in loads:
        load.start()
    for load in loads[:2]:
        load.wait()
    pl.semaphore_wait(barrier, len(friends))

    copies = {}

    def send(name, src, dst, target):
        k = len(copies)
        copy = pltpu.make_async_remote_copy(
            src_ref=src, dst_ref=dst, send_sem=send_sem.at[k], recv_sem=recv_sem.at[k],
            device_id=target, device_id_type=MESH,
        )
        copy.start()
        copies[name] = copy

    def got(*name):
        copies[name].wait_recv()

    weights = (wb, wk)

    def piece(w, zi, xi, row, rows):
        return weights[w].at[zlab[zi] * 4 + xlab[xi], pl.ds(row, rows)]

    def push(name, w, zi, xi, row, rows, target):
        ref = piece(w, zi, xi, row, rows)
        send(name, ref, ref, target)

    def z_step(w, base, xi, step):
        n = (w, base, xi)
        lower = pl.multiple_of(base + 32 * half, 32)
        upper = pl.multiple_of(base + 32 - 32 * half, 32)
        if step == 1:
            push(n + ("z1",), w, 0, xi, base, 64, outer)
        elif step == 2:
            got(*n, "z1")
            push(n + ("z2",), w, 1, xi, base, 64, inner)
        elif step == 3:
            got(*n, "z2")
            push(n + ("z3",), w, 2, xi, lower, 32, outer)
            if w == 0:
                push(n + ("z4",), w, 2, xi, lower, 32, outer_far)
        elif step == 4:
            got(*n, "z3")
            if w == 1:
                push(n + ("z4",), w, 3, xi, upper, 32, inner)
        else:
            got(*n, "z4")

    def x_step(w, base, zi, step, side):
        n = (w, base, zi, side)
        target = (right, left)[side]
        if step == 1:
            push(n + ("full",), w, zi, 0, base, 64, target)
        elif step == 2:
            got(*n, "full")
            push(n + ("half",), w, zi, 1 + side, base + 32 * side, 32, target)
        else:
            got(*n, "half")

    def share_tokens():
        loads[2].wait()
        for k in range(4):
            for s in range(16):
                xq[k, :, s * 128 : s * 128 + 128] = x_ref[:, s * 512 + k * 128 : s * 512 + k * 128 + 128]
        other = 2 - 2 * e
        send("x_near", xq.at[other + c], xr.at[2], ahead_same)
        send("x_cross", xq.at[other + 1 - c], xr.at[3], ahead_other)
        send("c_near", cots.at[0], cots.at[2], ahead_same)
        send("x_sib", xq.at[e * 2 + 1 - c], xr.at[1], sibling)
        send("c_sib", cots.at[0], cots.at[1], sibling)
        for load in loads[3:]:
            load.wait()

    def share_moments():
        for k in (1, 2, 3):
            for j in range(2):
                ref = mom.at[0, j, x]
                send(("m", 0, j, k), ref, ref, device(x + k, y, z, c))
                ref = mom.at[1, j, y]
                send(("m", 1, j, k), ref, ref, device(x, y + k, z, c))

    def forward_cotangent():
        copies["c_near"].wait_recv()
        send("c_cross", cots.at[2], cots.at[3], sibling)

    def project_group(zi):
        g = zlab[zi]
        columns = pl.ds(pl.multiple_of(g * 512, 512), 512)
        w = wb[pl.ds(g * 4, 4)].reshape(512, 512)
        return jnp.dot(xr[:, :, columns].reshape(512, 512), w, preferred_element_type=F32)

    def project_early():
        xr[0] = xq[q]
        for name in ("x_sib", "x_near", "x_cross"):
            copies[name].wait_recv()
        proj[...] = (project_group(0) + project_group(1)) + project_group(2)

    def project():
        pt[...] = (proj[...] + project_group(3)).T.astype(BF16)
        swapped[...] = jnp.dot(swap[...], pt[...], preferred_element_type=F32).astype(BF16)

    def prepare_swap():
        row = lax.broadcasted_iota(jnp.int32, (512, 512), 0)
        column = lax.broadcasted_iota(jnp.int32, (512, 512), 1)
        low, high = (row >> 1) & 3, row >> 7
        other_row = row + (low - high) * 126
        swap[...] = jnp.where(column == other_row, 1.0, 0.0).astype(BF16)
        basis_swapped[...] = jnp.dot(basis_ref[...], swap[...], preferred_element_type=F32).astype(BF16)

    def products(d):
        if d == 2:
            for name in ("c_sib", "c_cross"):
                copies[name].wait_recv()
        for at, matrix, columns in ((y, pt, left_half), (x, swapped, right_half)):
            rows = pl.ds(pl.multiple_of(((at + d) % 4) * 128, 128), 128)
            cot = cots[:, :, columns].reshape(512, 512)
            block = jnp.dot(matrix[rows, :], cot, preferred_element_type=F32)
            for k in range(2):
                pf[d, k, 0:32, columns] = block[k * 32 : k * 32 + 32]
                pf[d, k, 32:64, columns] = block[64 + k * 32 : 96 + k * 32]
        send(("s", d), pf.at[d, 1 - c], sib.at[d], sibling)

    def add_sibling(d):
        got("s", d)
        both = pf[d, c] + sib[d]
        if d == 0:
            ysum[...] = both
            return
        ysend[0, d - 1] = both[:, left_half].astype(BF16)
        ysend[1, d - 1] = both[:, right_half].astype(BF16)
        send(("y", 0, d), ysend.at[0, d - 1], yr.at[0, d - 1], device(x, y + d, z, c))
        send(("y", 1, d), ysend.at[1, d - 1], yr.at[1, d - 1], device(x + d, y, z, c))

    def grads(zi):
        g = zlab[zi]
        w = wk[pl.ds(g * 4, 4)].reshape(512, 1024)
        block = lax.dot_general(
            cots[...].reshape(512, 1024), w, (((1,), (1,)), ((), ())), preferred_element_type=F32
        ).astype(BF16)
        orecv[q, g] = block[0:128]
        for k in range(1, 4):
            osend[k - 1, zi] = block[k * 128 : k * 128 + 128]
        send(("o", 1, zi), osend.at[1, zi], orecv.at[q, g], behind_same)
        send(("o", 2, zi), osend.at[2, zi], orecv.at[q, g], ahead_other)
        send(("o", 0, zi), osend.at[0, zi], orecv.at[q, g], sibling)

    def add_y():
        for d in (1, 3, 2):
            got("y", 0, d)
            got("y", 1, d)
            ysum[...] += jnp.concatenate([yr[0, d - 1], yr[1, d - 1]], axis=1).astype(F32)
        for k in (4, 3, 5, 2, 6, 1, 7):
            zt = (z + k) % 8
            rows = ysum[pl.ds(pl.multiple_of((zt % 2) * 32 + (zt // 2) * 8, 8), 8), :]
            zsend[k - 1] = jnp.concatenate([rows[:, left_half], rows[:, right_half]], axis=0).astype(BF16)
            send(("z", k), zsend.at[k - 1], zr.at[k - 1], device(x, y, z + k, c))

    def add_z():
        total = ysum[pl.ds(pl.multiple_of(zl * 32 + zh * 8, 8), 8), :]
        for k in (1, 7, 2, 6, 3, 5, 4):
            got("z", k)
            rows = zr[k - 1].astype(F32)
            total += jnp.concatenate([rows[0:8], rows[8:16]], axis=1)
        xx[0, x] = total[:, left_half]
        xx[1, y] = total[:, right_half]
        for k in (2, 1, 3):
            send(("x", 0, k), xx.at[0, x], xx.at[0, x], device(x + k, y, z, c))
            send(("x", 1, k), xx.at[1, y], xx.at[1, y], device(x, y + k, z, c))

    def adam():
        for k in (1, 3, 2):
            for h in range(2):
                got("m", h, 0, k)
                got("m", h, 1, k)
                got("x", h, k)
        raw = jnp.concatenate([(xx[h, 0] + xx[h, 1]) + (xx[h, 2] + xx[h, 3]) for h in range(2)], axis=1)
        grad = SCALE * raw
        moment_first, moment_second = (
            jnp.concatenate(
                [jnp.concatenate([mom[h, j, k] for k in range(4)], axis=0) for h in range(2)], axis=1
            )
            for j in range(2)
        )
        first = 0.9 * moment_first + 0.1 * grad
        second = 0.999 * moment_second + 0.001 * grad * grad
        mean_hat = first / (1.0 - 0.9**STEP)
        var_hat = second / (1.0 - 0.999**STEP)
        direction = mean_hat / (jnp.sqrt(var_hat) + 1e-08)
        dz[z] = jnp.concatenate([direction[:, 0:512], direction[:, 512:1024]], axis=0).astype(BF16)
        for k in (4, 3, 5, 2, 6, 1, 7):
            send(("dz", k), dz.at[z], dz.at[z], device(x, y, z + k, c))
        for at, columns in ((x, left_half), (y, right_half)):
            picked = raw[0:2, columns]
            for k in range(1, 4):
                picked = jnp.where(at == k, raw[2 * k : 2 * k + 2, columns], picked)
            pg_ref[:, columns] = picked

    def gather_z():
        for k in (1, 7, 2, 6, 3, 5, 4):
            got("dz", k)
        for k in range(8):
            block = dz[k].astype(F32)
            row = (k % 2) * 32 + (k // 2) * 8
            d64[row : row + 8, 0:512] = block[0:8]
            d64[row : row + 8, 512:1024] = block[8:16]
        both = d64[...].astype(BF16)
        dall[0, y, c] = both[:, left_half]
        dall[1, x, c] = both[:, right_half]
        mine_left, mine_right = dall.at[0, y, c], dall.at[1, x, c]
        for k in (2, 1, 3):
            send(("dy", 0, k), mine_left, mine_left, device(x, y + k, z, c))
            send(("dy", 1, k), mine_right, mine_right, device(x + k, y, z, c))
        send(("ds", 0, 0), mine_left, mine_left, sibling)
        send(("ds", 1, 0), mine_right, mine_right, sibling)

    def collect(zi):
        for k in range(3):
            got("o", k, zi)
        g = zlab[zi]
        for k in range(4):
            for s in range(4):
                columns = pl.ds(pl.multiple_of(g * 2048 + s * 512 + k * 128, 128), 128)
                out_ref[:, columns] = orecv[k, g, :, s * 128 : s * 128 + 128]

    def update_part(shifts):
        products = []
        for h, (at, matrix) in enumerate(((y, basis_ref), (x, basis_swapped))):
            parts = [(at + k) % 4 for k in shifts]
            rows = [dall[h, i, k, zz * 32 : zz * 32 + 32] for i in parts for zz in range(2) for k in range(2)]
            columns = [matrix[:, pl.ds(pl.multiple_of(i * 128, 128), 128)] for i in parts]
            products.append(jnp.dot(
                jnp.concatenate(columns, axis=1), jnp.concatenate(rows, axis=0), preferred_element_type=F32
            ))
        return jnp.concatenate(products, axis=1)

    def forward_rows(k):
        for h, at in ((0, y), (1, x)):
            got("dy", h, k)
            block = dall.at[h, (at + 4 - k) % 4, c]
            send(("ds", h, k), block, block, sibling)

    def got_rows(k):
        got("ds", 0, k)
        got("ds", 1, k)

    def gather_y():
        forward_rows(1)
        forward_rows(3)
        for k in (0, 1, 3):
            got_rows(k)
        acc[...] = update_part([0, 3, 1])

    def update():
        forward_rows(2)
        got_rows(2)
        fu_ref[...] = (acc[...] + update_part([2])).astype(BF16)

    stages = {
        "z": z_step, "x": x_step, "o": grads, "tok": share_tokens,
        "cf": forward_cotangent, "mo": share_moments, "sw": prepare_swap, "pa": project_early, "pj": project, "pp": products, "as": add_sibling, "ay": add_y,
        "az": add_z, "ad": adam, "gz": gather_z, "co": collect, "gy": gather_y, "up": update,
    }
    sent = set()

    def settle(keep):
        for name in list(copies)[: len(copies) - keep]:
            if name not in sent:
                sent.add(name)
                copies[name].wait_send()

    for word, *where in SCHEDULE:
        stages[word](*where)
        if word in SETTLE:
            settle(24)
    settle(0)


COPIES = 176


def on_device(inputs, cotangent, kv_weight, basis, moment_first, moment_second):
    vmem = pl.BlockSpec(memory_space=pltpu.VMEM)
    shape = jax.ShapeDtypeStruct
    hbm = pl.BlockSpec(memory_space=pltpu.HBM)
    operands = [
        pltpu.with_memory_space_constraint(a, pltpu.HBM)
        for a in (inputs, cotangent, kv_weight, basis, moment_first, moment_second)
    ]
    input_grad, full_update, raw = pl.pallas_call(
        kernel,
        out_shape=(
            shape((128, 8192), BF16),
            shape((512, 1024), BF16),
            shape((2, 1024), F32),
        ),
        in_specs=[hbm] * 6,
        out_specs=[vmem] * 3,
        scratch_shapes=[
            pltpu.VMEM((128, 8192), BF16),
            pltpu.VMEM((512, 512), BF16),
            pltpu.VMEM((512, 512), BF16),
            pltpu.VMEM((512, 512), BF16),
            pltpu.VMEM((512, 512), BF16),
            pltpu.VMEM((512, 512), F32),
            pltpu.VMEM((512, 1024), F32),
            pltpu.VMEM((4, 128, 2048), BF16),
            pltpu.VMEM((4, 128, 2048), BF16),
            pltpu.VMEM((4, 128, 1024), BF16),
            pltpu.VMEM((16, 128, 512), BF16),
            pltpu.VMEM((16, 128, 1024), BF16),
            pltpu.VMEM((2, 2, 4, 2, 512), F32),
            pltpu.VMEM((512, 512), BF16),
            pltpu.VMEM((4, 2, 64, 1024), F32),
            pltpu.VMEM((4, 64, 1024), F32),
            pltpu.VMEM((64, 1024), F32),
            pltpu.VMEM((2, 3, 64, 512), BF16),
            pltpu.VMEM((2, 3, 64, 512), BF16),
            pltpu.VMEM((7, 16, 512), BF16),
            pltpu.VMEM((7, 16, 512), BF16),
            pltpu.VMEM((2, 4, 8, 512), F32),
            pltpu.VMEM((8, 16, 512), BF16),
            pltpu.VMEM((64, 1024), F32),
            pltpu.VMEM((2, 4, 2, 64, 512), BF16),
            pltpu.VMEM((3, 4, 128, 512), BF16),
            pltpu.VMEM((4, 4, 128, 512), BF16),
            pltpu.SemaphoreType.DMA((9,)),
            pltpu.SemaphoreType.DMA((COPIES,)),
            pltpu.SemaphoreType.DMA((COPIES,)),
        ],
        compiler_params=pltpu.CompilerParams(
            collective_id=0, has_side_effects=True, vmem_limit_bytes=48 << 20
        ),
    )(*operands)
    proj_grad = SCALE * raw
    first_new = 0.9 * moment_first + 0.1 * proj_grad
    second_new = 0.999 * moment_second + 0.001 * proj_grad * proj_grad
    return input_grad, full_update, proj_grad, first_new, second_new


def solution(mesh):
    tokens = P(("rep", "dp"), None)
    shard = P("dp", None)
    return jax.shard_map(
        on_device,
        mesh=mesh,
        in_specs=(tokens, tokens, shard, shard, tokens, tokens),
        out_specs=(tokens, shard, tokens, tokens, tokens),
        check_vma=False,
    )
```

```python
import functools

import jax
import jax.numpy as jnp
from jax import lax
from jax.experimental import pallas as pl
from jax.experimental.pallas import tpu as pltpu
from jax.sharding import PartitionSpec as P

MESH = pl.DeviceIdType.MESH
STEP = 20
TOKENS = 32768
F32 = jnp.float32
BF16 = jnp.bfloat16
SCALE = float(TOKENS) ** -0.5
SCHEDULE = (
    ("z", 0, 0, 0, 1), ("x", 0, 64, 0, 1, 1), ("x", 0, 64, 0, 1, 0), ("tok",), ("x", 0, 0, 0, 1, 1),
    ("x", 0, 0, 0, 1, 0), ("z", 0, 64, 0, 1), ("z", 0, 0, 0, 2), ("x", 0, 64, 0, 2, 1),
    ("x", 0, 64, 0, 2, 0), ("z", 0, 64, 2, 1), ("x", 0, 0, 1, 1, 0), ("z", 0, 64, 1, 1),
    ("x", 0, 0, 1, 1, 1), ("sw",), ("x", 0, 0, 0, 2, 1), ("z", 0, 64, 0, 2), ("x", 0, 0, 0, 2, 0),
    ("x", 0, 64, 0, 3, 1), ("x", 0, 64, 0, 3, 0), ("z", 0, 64, 3, 1), ("z", 0, 0, 0, 3),
    ("x", 0, 0, 2, 1, 0), ("x", 0, 0, 2, 1, 1), ("z", 0, 64, 2, 2), ("x", 0, 0, 1, 2, 0),
    ("x", 0, 0, 1, 2, 1), ("x", 0, 0, 0, 3, 1), ("z", 0, 64, 1, 2), ("x", 0, 0, 0, 3, 0), ("z", 0, 64, 0, 3),
    ("z", 0, 64, 3, 2), ("x", 0, 0, 2, 2, 0), ("x", 0, 0, 2, 2, 1), ("z", 0, 64, 2, 3), ("x", 0, 0, 1, 3, 0),
    ("z", 0, 0, 0, 4), ("x", 0, 0, 1, 3, 1), ("z", 0, 0, 0, 5), ("x", 0, 0, 3, 1, 0), ("z", 0, 64, 1, 3),
    ("x", 0, 0, 3, 1, 1), ("z", 0, 64, 0, 4), ("x", 1, 64, 0, 1, 0), ("z", 1, 64, 0, 1), ("z", 0, 64, 0, 5),
    ("x", 1, 64, 0, 1, 1), ("x", 0, 0, 2, 3, 0), ("z", 0, 64, 3, 3), ("x", 0, 0, 2, 3, 1), ("pa",),
    ("z", 0, 64, 1, 4), ("z", 0, 64, 2, 4), ("cf",), ("x", 0, 0, 3, 2, 0), ("x", 0, 0, 3, 2, 1),
    ("z", 0, 64, 2, 5), ("mo",), ("z", 0, 64, 1, 5), ("z", 1, 0, 0, 1), ("x", 1, 0, 0, 1, 1),
    ("x", 1, 0, 0, 1, 0), ("z", 1, 64, 0, 2), ("x", 0, 0, 3, 3, 0), ("z", 0, 64, 3, 4), ("x", 0, 0, 3, 3, 1),
    ("x", 1, 64, 0, 2, 1), ("x", 1, 64, 0, 2, 0), ("z", 1, 64, 2, 1), ("z", 0, 64, 3, 5), ("pj",), ("pp", 2),
    ("pp", 1), ("pp", 3), ("pp", 0), ("as", 2), ("as", 1), ("x", 1, 64, 0, 3, 1), ("z", 1, 0, 0, 2),
    ("as", 3), ("x", 1, 64, 0, 3, 0), ("z", 1, 64, 1, 1), ("as", 0), ("x", 1, 0, 1, 1, 1),
    ("x", 1, 0, 1, 1, 0), ("z", 1, 64, 2, 2), ("z", 1, 64, 3, 1), ("x", 1, 0, 0, 2, 1), ("x", 1, 0, 0, 2, 0),
    ("ay",), ("z", 1, 0, 0, 3), ("x", 1, 0, 2, 1, 1), ("x", 1, 0, 2, 1, 0), ("z", 1, 64, 1, 2),
    ("z", 1, 64, 0, 3), ("x", 1, 0, 0, 3, 0), ("x", 1, 0, 0, 3, 1), ("o", 0), ("x", 1, 0, 1, 2, 1),
    ("x", 1, 0, 1, 2, 0), ("z", 1, 64, 2, 3), ("z", 1, 0, 0, 4), ("az",), ("z", 1, 64, 3, 2),
    ("x", 1, 0, 2, 2, 1), ("x", 1, 0, 2, 2, 0), ("z", 1, 64, 1, 3), ("x", 1, 0, 1, 3, 1),
    ("x", 1, 0, 1, 3, 0), ("o", 1), ("z", 1, 0, 0, 5), ("x", 1, 0, 3, 1, 0), ("x", 1, 0, 3, 1, 1), ("ad",),
    ("co", 0), ("x", 1, 0, 2, 3, 1), ("x", 1, 0, 2, 3, 0), ("z", 1, 64, 1, 4), ("z", 1, 64, 3, 3), ("o", 2),
    ("z", 1, 64, 0, 4), ("z", 1, 64, 2, 4), ("co", 1), ("x", 1, 0, 3, 2, 0), ("x", 1, 0, 3, 2, 1),
    ("z", 1, 64, 1, 5), ("z", 1, 64, 3, 4), ("gz",), ("z", 1, 64, 0, 5), ("co", 2), ("z", 1, 64, 2, 5),
    ("x", 1, 0, 3, 3, 0), ("x", 1, 0, 3, 3, 1), ("z", 1, 64, 3, 5), ("o", 3), ("gy",), ("up",), ("co", 3),
)
SETTLE = ("as", "ay", "az", "ad", "gz")


def device(x, y, z, c):
    return ((y % 4) * 4 + (z % 2) * 2 + c, ((z % 8) // 2) * 4 + x % 4)


def kernel(
    x_hbm, cot_hbm, kv_hbm, basis_hbm, m1_hbm, m2_hbm,
    out_ref, fu_ref, pg_ref,
    x_ref, basis_ref, basis_swapped, swap, swapped, proj, acc, xq, xr, cots, wb, wk, mom, pt, pf, sib, ysum, ysend, yr, zsend, zr, xx, dz, d64, dall, osend, orecv,
    load_sem, send_sem, recv_sem,
):
    rep, dp = lax.axis_index("rep"), lax.axis_index("dp")
    c, zl, y = rep % 2, (rep // 2) % 2, rep // 4
    zh, x = dp // 4, dp % 4
    z = zh * 2 + zl
    e = y % 2
    q = e * 2 + c
    dy = 1 - 2 * c + 4
    sigma = 2 * zl - 1 + 4
    half = 1 - zl
    zlab = [zh, (zh + sigma) % 4, (zh + 8 - sigma) % 4, (zh + 2) % 4]
    xlab = [x, (x + 3) % 4, (x + 1) % 4, (x + 2) % 4]
    outer = device(x, y, z + 8 + 2 * zl - 1, c)
    inner = device(x, y, z + 1 - 2 * zl, c)
    outer_far = device(x, y, z + 8 + 4 * zl - 2, c)
    right, left = device(x + 1, y, z, c), device(x + 3, y, z, c)
    sibling = device(x, y, z, 1 - c)
    left_half, right_half = slice(0, 512), slice(512, 1024)
    ahead_same = device(x, y + dy, z, c)
    ahead_other = device(x, y + dy, z, 1 - c)
    behind_same = device(x, y + 8 - dy, z, c)
    behind_other = device(x, y + 8 - dy, z, 1 - c)

    barrier = pltpu.get_barrier_semaphore()
    friends = [sibling, ahead_same, ahead_other, behind_same, behind_other]
    friends += [right, left, outer, inner]
    for friend in friends:
        pl.semaphore_signal(barrier, inc=1, device_id=friend, device_id_type=MESH)

    mine = zh * 4 + x
    quarter = pl.ds(pl.multiple_of(q * 128, 128), 128)
    loads = [
        pltpu.make_async_copy(src, dst, load_sem.at[k])
        for k, (src, dst) in enumerate((
            (basis_hbm.at[quarter], wb.at[mine]),
            (cot_hbm, cots.at[0]),
            (x_hbm, x_ref),
            (kv_hbm.at[quarter], wk.at[mine]),
            (m1_hbm.at[:, pl.ds(0, 512)], mom.at[0, 0, x]),
            (m1_hbm.at[:, pl.ds(512, 512)], mom.at[1, 0, y]),
            (m2_hbm.at[:, pl.ds(0, 512)], mom.at[0, 1, x]),
            (m2_hbm.at[:, pl.ds(512, 512)], mom.at[1, 1, y]),
            (basis_hbm, basis_ref),
        ))
    ]
    for load in loads:
        load.start()
    for load in loads[:2]:
        load.wait()
    pl.semaphore_wait(barrier, len(friends))

    copies = {}

    def send(name, src, dst, target):
        k = len(copies)
        copy = pltpu.make_async_remote_copy(
            src_ref=src, dst_ref=dst, send_sem=send_sem.at[k], recv_sem=recv_sem.at[k],
            device_id=target, device_id_type=MESH,
        )
        copy.start()
        copies[name] = copy

    def got(*name):
        copies[name].wait_recv()

    weights = (wb, wk)

    def piece(w, zi, xi, row, rows):
        return weights[w].at[zlab[zi] * 4 + xlab[xi], pl.ds(row, rows)]

    def push(name, w, zi, xi, row, rows, target):
        ref = piece(w, zi, xi, row, rows)
        send(name, ref, ref, target)

    def z_step(w, base, xi, step):
        n = (w, base, xi)
        lower = pl.multiple_of(base + 32 * half, 32)
        upper = pl.multiple_of(base + 32 - 32 * half, 32)
        if step == 1:
            push(n + ("z1",), w, 0, xi, base, 64, outer)
        elif step == 2:
            got(*n, "z1")
            push(n + ("z2",), w, 1, xi, base, 64, inner)
        elif step == 3:
            got(*n, "z2")
            push(n + ("z3",), w, 2, xi, lower, 32, outer)
            if w == 0:
                push(n + ("z4",), w, 2, xi, lower, 32, outer_far)
        elif step == 4:
            got(*n, "z3")
            if w == 1:
                push(n + ("z4",), w, 3, xi, upper, 32, inner)
        else:
            got(*n, "z4")

    def x_step(w, base, zi, step, side):
        n = (w, base, zi, side)
        target = (right, left)[side]
        if step == 1:
            push(n + ("full",), w, zi, 0, base, 64, target)
        elif step == 2:
            got(*n, "full")
            push(n + ("half",), w, zi, 1 + side, base + 32 * side, 32, target)
        else:
            got(*n, "half")

    def share_tokens():
        loads[2].wait()
        for k in range(4):
            for s in range(16):
                xq[k, :, s * 128 : s * 128 + 128] = x_ref[:, s * 512 + k * 128 : s * 512 + k * 128 + 128]
        other = 2 - 2 * e
        send("x_near", xq.at[other + c], xr.at[2], ahead_same)
        send("x_cross", xq.at[other + 1 - c], xr.at[3], ahead_other)
        send("c_near", cots.at[0], cots.at[2], ahead_same)
        send("x_sib", xq.at[e * 2 + 1 - c], xr.at[1], sibling)
        send("c_sib", cots.at[0], cots.at[1], sibling)
        for load in loads[3:]:
            load.wait()

    def share_moments():
        for k in (1, 2, 3):
            for j in range(2):
                ref = mom.at[0, j, x]
                send(("m", 0, j, k), ref, ref, device(x + k, y, z, c))
                ref = mom.at[1, j, y]
                send(("m", 1, j, k), ref, ref, device(x, y + k, z, c))

    def forward_cotangent():
        copies["c_near"].wait_recv()
        send("c_cross", cots.at[2], cots.at[3], sibling)

    def project_group(zi):
        g = zlab[zi]
        columns = pl.ds(pl.multiple_of(g * 512, 512), 512)
        w = wb[pl.ds(g * 4, 4)].reshape(512, 512)
        return jnp.dot(xr[:, :, columns].reshape(512, 512), w, preferred_element_type=F32)

    def project_early():
        xr[0] = xq[q]
        for name in ("x_sib", "x_near", "x_cross"):
            copies[name].wait_recv()
        proj[...] = (project_group(0) + project_group(1)) + project_group(2)

    def project():
        pt[...] = (proj[...] + project_group(3)).astype(BF16).T
        swapped[...] = jnp.dot(swap[...], pt[...], preferred_element_type=F32).astype(BF16)

    def prepare_swap():
        row = lax.broadcasted_iota(jnp.int32, (512, 512), 0)
        column = lax.broadcasted_iota(jnp.int32, (512, 512), 1)
        low, high = (row >> 1) & 3, row >> 7
        other_row = row + (low - high) * 126
        swap[...] = jnp.where(column == other_row, 1.0, 0.0).astype(BF16)
        basis_swapped[...] = jnp.dot(basis_ref[...], swap[...], preferred_element_type=F32).astype(BF16)

    def products(d):
        if d == 2:
            for name in ("c_sib", "c_cross"):
                copies[name].wait_recv()
        for at, matrix, columns in ((y, pt, left_half), (x, swapped, right_half)):
            rows = pl.ds(pl.multiple_of(((at + d) % 4) * 128, 128), 128)
            cot = cots[:, :, columns].reshape(512, 512)
            block = jnp.dot(matrix[rows, :], cot, preferred_element_type=F32)
            for k in range(2):
                pf[d, k, 0:32, columns] = block[k * 32 : k * 32 + 32]
                pf[d, k, 32:64, columns] = block[64 + k * 32 : 96 + k * 32]
        send(("s", d), pf.at[d, 1 - c], sib.at[d], sibling)

    def add_sibling(d):
        got("s", d)
        both = pf[d, c] + sib[d]
        if d == 0:
            ysum[...] = both
            return
        ysend[0, d - 1] = both[:, left_half].astype(BF16)
        ysend[1, d - 1] = both[:, right_half].astype(BF16)
        send(("y", 0, d), ysend.at[0, d - 1], yr.at[0, d - 1], device(x, y + d, z, c))
        send(("y", 1, d), ysend.at[1, d - 1], yr.at[1, d - 1], device(x + d, y, z, c))

    def grads(zi):
        g = zlab[zi]
        w = wk[pl.ds(g * 4, 4)].reshape(512, 1024)
        block = lax.dot_general(
            cots[...].reshape(512, 1024), w, (((1,), (1,)), ((), ())), preferred_element_type=F32
        ).astype(BF16)
        orecv[q, g] = block[0:128]
        for k in range(1, 4):
            osend[k - 1, zi] = block[k * 128 : k * 128 + 128]
        send(("o", 1, zi), osend.at[1, zi], orecv.at[q, g], behind_same)
        send(("o", 2, zi), osend.at[2, zi], orecv.at[q, g], ahead_other)
        send(("o", 0, zi), osend.at[0, zi], orecv.at[q, g], sibling)

    def add_y():
        for d in (1, 3, 2):
            got("y", 0, d)
            got("y", 1, d)
            ysum[...] += jnp.concatenate([yr[0, d - 1], yr[1, d - 1]], axis=1).astype(F32)
        for k in (4, 3, 5, 2, 6, 1, 7):
            zt = (z + k) % 8
            rows = ysum[pl.ds(pl.multiple_of((zt % 2) * 32 + (zt // 2) * 8, 8), 8), :]
            zsend[k - 1] = jnp.concatenate([rows[:, left_half], rows[:, right_half]], axis=0).astype(BF16)
            send(("z", k), zsend.at[k - 1], zr.at[k - 1], device(x, y, z + k, c))

    def add_z():
        total = ysum[pl.ds(pl.multiple_of(zl * 32 + zh * 8, 8), 8), :]
        for k in (1, 7, 2, 6, 3, 5, 4):
            got("z", k)
            rows = zr[k - 1].astype(F32)
            total += jnp.concatenate([rows[0:8], rows[8:16]], axis=1)
        xx[0, x] = total[:, left_half]
        xx[1, y] = total[:, right_half]
        for k in (2, 1, 3):
            send(("x", 0, k), xx.at[0, x], xx.at[0, x], device(x + k, y, z, c))
            send(("x", 1, k), xx.at[1, y], xx.at[1, y], device(x, y + k, z, c))

    def adam():
        for k in (1, 3, 2):
            for h in range(2):
                got("m", h, 0, k)
                got("m", h, 1, k)
                got("x", h, k)
        raw = jnp.concatenate([(xx[h, 0] + xx[h, 1]) + (xx[h, 2] + xx[h, 3]) for h in range(2)], axis=1)
        grad = SCALE * raw
        moment_first, moment_second = (
            jnp.concatenate(
                [jnp.concatenate([mom[h, j, k] for k in range(4)], axis=0) for h in range(2)], axis=1
            )
            for j in range(2)
        )
        first = 0.9 * moment_first + 0.1 * grad
        second = 0.999 * moment_second + 0.001 * grad * grad
        mean_hat = first / (1.0 - 0.9**STEP)
        var_hat = second / (1.0 - 0.999**STEP)
        direction = mean_hat / (jnp.sqrt(var_hat) + 1e-08)
        dz[z] = jnp.concatenate([direction[:, 0:512], direction[:, 512:1024]], axis=0).astype(BF16)
        for k in (4, 3, 5, 2, 6, 1, 7):
            send(("dz", k), dz.at[z], dz.at[z], device(x, y, z + k, c))
        for at, columns in ((x, left_half), (y, right_half)):
            picked = raw[0:2, columns]
            for k in range(1, 4):
                picked = jnp.where(at == k, raw[2 * k : 2 * k + 2, columns], picked)
            pg_ref[:, columns] = picked

    def gather_z():
        for k in (1, 7, 2, 6, 3, 5, 4):
            got("dz", k)
        for k in range(8):
            block = dz[k].astype(F32)
            row = (k % 2) * 32 + (k // 2) * 8
            d64[row : row + 8, 0:512] = block[0:8]
            d64[row : row + 8, 512:1024] = block[8:16]
        both = d64[...].astype(BF16)
        dall[0, y, c] = both[:, left_half]
        dall[1, x, c] = both[:, right_half]
        mine_left, mine_right = dall.at[0, y, c], dall.at[1, x, c]
        for k in (2, 1, 3):
            send(("dy", 0, k), mine_left, mine_left, device(x, y + k, z, c))
            send(("dy", 1, k), mine_right, mine_right, device(x + k, y, z, c))
        send(("ds", 0, 0), mine_left, mine_left, sibling)
        send(("ds", 1, 0), mine_right, mine_right, sibling)

    def collect(zi):
        for k in range(3):
            got("o", k, zi)
        g = zlab[zi]
        for k in range(4):
            for s in range(4):
                columns = pl.ds(pl.multiple_of(g * 2048 + s * 512 + k * 128, 128), 128)
                out_ref[:, columns] = orecv[k, g, :, s * 128 : s * 128 + 128]

    def update_part(shifts):
        products = []
        for h, (at, matrix) in enumerate(((y, basis_ref), (x, basis_swapped))):
            parts = [(at + k) % 4 for k in shifts]
            rows = [dall[h, i, k, zz * 32 : zz * 32 + 32] for i in parts for zz in range(2) for k in range(2)]
            columns = [matrix[:, pl.ds(pl.multiple_of(i * 128, 128), 128)] for i in parts]
            products.append(jnp.dot(
                jnp.concatenate(columns, axis=1), jnp.concatenate(rows, axis=0), preferred_element_type=F32
            ))
        return jnp.concatenate(products, axis=1)

    def forward_rows(k):
        for h, at in ((0, y), (1, x)):
            got("dy", h, k)
            block = dall.at[h, (at + 4 - k) % 4, c]
            send(("ds", h, k), block, block, sibling)

    def got_rows(k):
        got("ds", 0, k)
        got("ds", 1, k)

    def gather_y():
        forward_rows(1)
        forward_rows(3)
        for k in (0, 1, 3):
            got_rows(k)
        acc[...] = update_part([0, 3, 1])

    def update():
        forward_rows(2)
        got_rows(2)
        fu_ref[...] = (acc[...] + update_part([2])).astype(BF16)

    stages = {
        "z": z_step, "x": x_step, "o": grads, "tok": share_tokens,
        "cf": forward_cotangent, "mo": share_moments, "sw": prepare_swap, "pa": project_early, "pj": project, "pp": products, "as": add_sibling, "ay": add_y,
        "az": add_z, "ad": adam, "gz": gather_z, "co": collect, "gy": gather_y, "up": update,
    }
    sent = set()

    def settle(keep):
        for name in list(copies)[: len(copies) - keep]:
            if name not in sent:
                sent.add(name)
                copies[name].wait_send()

    for word, *where in SCHEDULE:
        stages[word](*where)
        if word in SETTLE:
            settle(24)
    settle(0)


COPIES = 176


def on_device(inputs, cotangent, kv_weight, basis, moment_first, moment_second):
    vmem = pl.BlockSpec(memory_space=pltpu.VMEM)
    shape = jax.ShapeDtypeStruct
    hbm = pl.BlockSpec(memory_space=pltpu.HBM)
    operands = [
        pltpu.with_memory_space_constraint(a, pltpu.HBM)
        for a in (inputs, cotangent, kv_weight, basis, moment_first, moment_second)
    ]
    input_grad, full_update, raw = pl.pallas_call(
        kernel,
        out_shape=(
            shape((128, 8192), BF16),
            shape((512, 1024), BF16),
            shape((2, 1024), F32),
        ),
        in_specs=[hbm] * 6,
        out_specs=[vmem] * 3,
        scratch_shapes=[
            pltpu.VMEM((128, 8192), BF16),
            pltpu.VMEM((512, 512), BF16),
            pltpu.VMEM((512, 512), BF16),
            pltpu.VMEM((512, 512), BF16),
            pltpu.VMEM((512, 512), BF16),
            pltpu.VMEM((512, 512), F32),
            pltpu.VMEM((512, 1024), F32),
            pltpu.VMEM((4, 128, 2048), BF16),
            pltpu.VMEM((4, 128, 2048), BF16),
            pltpu.VMEM((4, 128, 1024), BF16),
            pltpu.VMEM((16, 128, 512), BF16),
            pltpu.VMEM((16, 128, 1024), BF16),
            pltpu.VMEM((2, 2, 4, 2, 512), F32),
            pltpu.VMEM((512, 512), BF16),
            pltpu.VMEM((4, 2, 64, 1024), F32),
            pltpu.VMEM((4, 64, 1024), F32),
            pltpu.VMEM((64, 1024), F32),
            pltpu.VMEM((2, 3, 64, 512), BF16),
            pltpu.VMEM((2, 3, 64, 512), BF16),
            pltpu.VMEM((7, 16, 512), BF16),
            pltpu.VMEM((7, 16, 512), BF16),
            pltpu.VMEM((2, 4, 8, 512), F32),
            pltpu.VMEM((8, 16, 512), BF16),
            pltpu.VMEM((64, 1024), F32),
            pltpu.VMEM((2, 4, 2, 64, 512), BF16),
            pltpu.VMEM((3, 4, 128, 512), BF16),
            pltpu.VMEM((4, 4, 128, 512), BF16),
            pltpu.SemaphoreType.DMA((9,)),
            pltpu.SemaphoreType.DMA((COPIES,)),
            pltpu.SemaphoreType.DMA((COPIES,)),
        ],
        compiler_params=pltpu.CompilerParams(
            collective_id=0, has_side_effects=True, vmem_limit_bytes=48 << 20
        ),
    )(*operands)
    proj_grad = SCALE * raw
    first_new = 0.9 * moment_first + 0.1 * proj_grad
    second_new = 0.999 * moment_second + 0.001 * proj_grad * proj_grad
    return input_grad, full_update, proj_grad, first_new, second_new


def solution(mesh):
    tokens = P(("rep", "dp"), None)
    shard = P("dp", None)
    return jax.shard_map(
        on_device,
        mesh=mesh,
        in_specs=(tokens, tokens, shard, shard, tokens, tokens),
        out_specs=(tokens, shard, tokens, tokens, tokens),
        check_vma=False,
    )
```
